256 devices in a mesh: pool: 2 (over core), grp: 8 (over x_hi, y), tp: 16 (over x_lo, z).
Axes of the slice: x: 4 (x_hi: 2, x_lo: 2; x = x_hi * 2 + x_lo), y: 4, z: 8, core: 2. Of those that a mesh axis runs over, the one named last changes fastest.
Arguments:
- hidden_rows: bfloat16 [2, 8192, 8192], P('pool', ('grp', 'tp')), may hold values from -17 to 17
- w_query: bfloat16 [8192, 8192], P(None, 'tp'), may hold values from -0.0625 to 0.0625
- key_matrix: bfloat16 [8192, 1024], P(None, 'tp'), may hold values from -0.0625 to 0.0625
- value_matrix: bfloat16 [8192, 1024], P(None, 'tp'), may hold values from -0.0625 to 0.0625
- resident_cache: bfloat16 [4096, 16, 4096], P('grp', None, 'tp'), may hold values from -6 to 6
- page_req: int32 [512], P('grp'), may hold values from 0 to 64, as said below
- req_len: int32 [64], replicated, may hold values from 1 to 128, as said below
- assign: int32 [64], replicated, may hold values from 0 to 7, as said below
- row_src: int32 [2048], P('grp'), may hold values from 0 to 7
- resident_length: int32 [2048], P('grp'), may hold values from 1 to 32
- page_lookup: int32 [2048, 2], P('grp'), may hold values from 0 to 511, as said below
Outputs:
- attended: bfloat16 [2, 8192, 8192], P('pool', 'grp', 'tp')
The draws below stay inside these ranges and needn't reach their ends.
Inputs may be any that keep to these rules, and one draw needn't show every extreme that they name: `page_req`: requests g * 8 to g * 8 + 7 belong to prefill group g and take its pages in that order from its first page, each 1 to 8 consecutive pages; the pages after them carry 64. `req_len`: A request of c pages has between (c - 1) * 16 + 1 and c * 16 tokens. `assign`: the 8 requests of one prefill group go to 8 different decode groups. `page_lookup`: the entries of all rows of one decode group are distinct.
All inputs are finite; a program needn't handle non-finite values.
Results may differ from the reference program's by a relative error of at most 0.012.
Values may be sent and summed in bfloat16 or wider, within the bound.
No kernel may reach another device: no remote copies, remote signals or barrier semaphores. Data moves between devices by JAX's collectives and lax.ppermute only.
A program may use at most 128 MiB of HBM per device.

```python
import math
import jax
import jax.numpy as jnp
from jax import lax

MODEL_WIDTH = 8192
KEY_VALUE_HEADS = 8
HEAD_SIZE = 128
QUERY_HEADS = 64
PAGE_TOKENS = 16
DECODE_STEPS = 4
ROW_PAGE_LIMIT = 2
GROUP_ROWS = 1024
POOL_ROWS = 8192
PPG = 64
NREQ = 64
MOSTP = 8
DECODE_GROUPROWS = 256
GROUP_PAGES = 512
QHD = 4
REP = 2
KVN = 1
CACHE_WIDTH = 4096
N_GRP = 8
N_TP = 16


def request_layout(key):
    count_key, forced_key, tail_key, order_key, target_key = jax.random.split(key, 5)
    slots = jnp.arange(N_GRP, dtype=jnp.int32)
    counts = jax.random.randint(count_key, (N_GRP, N_GRP), 1, MOSTP + 1)
    forced = jax.random.randint(forced_key, (N_GRP,), 0, N_GRP)
    chosen = slots[None, :] == forced[:, None]
    counts = jnp.where(chosen, MOSTP, counts)
    tails = jnp.where(chosen, PAGE_TOKENS, jax.random.randint(tail_key, (N_GRP, N_GRP), 1, PAGE_TOKENS + 1))
    lengths = (counts - 1) * PAGE_TOKENS + tails
    orders = jax.vmap(lambda part_key: jax.random.permutation(part_key, N_GRP))(jax.random.split(order_key, N_GRP))
    target = jax.random.randint(target_key, (), 0, N_GRP)
    pinned = jnp.take_along_axis(orders, forced[:, None], axis=1)
    assigned = jnp.mod(orders - pinned + target, N_GRP)
    ends = jnp.cumsum(counts, axis=1)
    pages = jnp.arange(PPG, dtype=jnp.int32)
    local = jnp.sum((pages[None, :, None] >= ends[:, None, :]).astype(jnp.int32), axis=2)
    owner_list = jnp.where(local < N_GRP, slots[:, None] * N_GRP + local, NREQ)
    return (owner_list.reshape(-1).astype(jnp.int32), lengths.reshape(-1).astype(jnp.int32), assigned.reshape(-1).astype(jnp.int32))


def draw_page_req(key, part):
    return request_layout(key)[0]


def draw_req_len(key, part):
    return request_layout(key)[1]


def draw_assign(key, part):
    return request_layout(key)[2]


def draw_hidden_rows(key, part):
    key = jax.random.fold_in(key, 13)
    base_key = jax.random.fold_in(key, 0)
    shape = (2, POOL_ROWS, MODEL_WIDTH)
    value_rows = jnp.clip(jax.random.normal(base_key, shape, jnp.float32), -5.0, 5.0)
    return value_rows.astype(jnp.bfloat16)


def draw_resident_length(key, part):
    key = jax.random.fold_in(key, 11)
    value_key, chosen_key = jax.random.split(key)
    count = N_GRP * DECODE_GROUPROWS
    longest = ROW_PAGE_LIMIT * PAGE_TOKENS
    value_rows = jax.random.randint(value_key, (count,), 1, longest + 1)
    chosen = jax.random.randint(chosen_key, (), 0, count)
    return jnp.where(jnp.arange(count) == chosen, longest, value_rows).astype(jnp.int32)


def draw_page_lookup(key, part):
    key = jax.random.fold_in(key, 12)
    tables = jax.vmap(lambda part_key: jax.random.permutation(part_key, GROUP_PAGES))(jax.random.split(key, N_GRP))
    return tables.reshape(N_GRP * DECODE_GROUPROWS, ROW_PAGE_LIMIT).astype(jnp.int32)


def with_ends(entries, rng, least, largest):
    extent = entries.shape
    spot = [jax.random.randint(jax.random.fold_in(rng, axis), (), 0, extent[axis]) for axis in range(len(extent))]
    entries = entries.at[tuple(spot)].set(least)
    longest = extent.index(max(extent))
    spot[longest] = (spot[longest] + 1) % extent[longest]
    return entries.at[tuple(spot)].set(largest)


def block_levels(rng, extent, cuts, least, high):
    def one(position, shards_of):
        heights = jax.random.uniform(jax.random.fold_in(jax.random.fold_in(rng, 6), position), (shards_of,), jnp.float32, least / len(cuts), high / len(cuts))
        return jnp.repeat(jnp.exp(heights), extent[position] // shards_of).reshape((-1,) + (1,) * (len(extent) - position - 1))

    loudness = one(*cuts[0])
    for cut in cuts[1:]:
        loudness = loudness * one(*cut)
    return loudness


def noise(stream_key, shape, scale, limit, cuts=(), held_as=jnp.bfloat16):
    result = scale * jax.random.normal(stream_key, shape, jnp.float32)
    if cuts:
        result = result * block_levels(stream_key, shape, cuts, -0.22, 0.18)
    return jnp.clip(result, -limit, limit).astype(held_as)


def setup_inputs(seed: int = 0) -> dict:
    key_list = jax.random.split(jax.random.key(seed), 12)
    return {
        "hidden_rows": draw_hidden_rows(jax.random.fold_in(key_list[11], 71), 0),
        "w_query": noise(key_list[1], (MODEL_WIDTH, QUERY_HEADS * HEAD_SIZE), MODEL_WIDTH ** -0.5, 0.0625, ((1, 16),)),
        "key_matrix": noise(key_list[2], (MODEL_WIDTH, KEY_VALUE_HEADS * HEAD_SIZE), MODEL_WIDTH ** -0.5, 0.0625, ((1, 16),)),
        "value_matrix": noise(key_list[3], (MODEL_WIDTH, KEY_VALUE_HEADS * HEAD_SIZE), MODEL_WIDTH ** -0.5, 0.0625, ((1, 16),)),
        "resident_cache": noise(key_list[4], (N_GRP * GROUP_PAGES, PAGE_TOKENS, CACHE_WIDTH), 1.0, 6.0, ((0, 8), (2, 16))),
        "page_req": draw_page_req(jax.random.fold_in(key_list[11], 71), 0),
        "req_len": draw_req_len(jax.random.fold_in(key_list[11], 71), 0),
        "assign": draw_assign(jax.random.fold_in(key_list[11], 71), 0),
        "row_src": with_ends(jax.random.randint(key_list[8], (N_GRP * DECODE_GROUPROWS,), 0, N_GRP), jax.random.fold_in(key_list[8], 1), 0, N_GRP - 1).astype(jnp.int32),
        "resident_length": draw_resident_length(jax.random.fold_in(key_list[11], 71), 0),
        "page_lookup": draw_page_lookup(jax.random.fold_in(key_list[11], 71), 0),
    }


theta_base = 500000.0
masked_score = -1e30


def rotate(value_rows, place_list, width):
    count = value_rows.shape[0]
    heads = value_rows.reshape(count, -1, width)
    half = width // 2
    freqs = jnp.exp(jnp.arange(half, dtype=jnp.float32) * (-2.0 * math.log(theta_base) / width))
    angles = place_list.astype(jnp.float32)[:, None] * freqs[None, :]
    cosine = jnp.cos(angles)[:, None, :]
    sine = jnp.sin(angles)[:, None, :]
    first = heads[:, :, :half]
    second = heads[:, :, half:]
    turned = jnp.concatenate([first * cosine - second * sine, second * cosine + first * sine], axis=2)
    return turned.reshape(count, -1)


def normalize(scores):
    summit = jnp.max(scores, axis=-1, keepdims=True)
    expsum = jnp.exp(scores - summit)
    return (expsum / jnp.sum(expsum, axis=-1, keepdims=True)).astype(jnp.bfloat16)


def prefill_layout(page_req, req_len, page):
    count = page_req.shape[0]
    index = jnp.arange(count, dtype=jnp.int32)
    same = page_req[:, None] == page_req[None, :]
    first = jnp.min(jnp.where(same, index[None, :], count), axis=1)
    owner_list = jnp.repeat(page_req, page)
    place_list = jnp.arange(count * page, dtype=jnp.int32) - jnp.repeat(first, page) * page
    match = owner_list[:, None] == jnp.arange(req_len.shape[0], dtype=jnp.int32)[None, :]
    lengths = jnp.sum(jnp.where(match, req_len[None, :], 0), axis=1)
    return owner_list, place_list, place_list < lengths


def decode_layout(row_src, assign, req_len, group_index, groups):
    slots = jnp.arange(groups, dtype=jnp.int32)
    table = assign.reshape(groups, groups)
    chosen = jnp.sum(jnp.where(table == group_index, slots[None, :], 0), axis=1)
    requests = slots * groups + chosen
    catalog = jnp.arange(req_len.shape[0], dtype=jnp.int32)
    lengths = jnp.sum(jnp.where(requests[:, None] == catalog[None, :], req_len[None, :], 0), axis=1)
    pick = row_src[:, None] == slots[None, :]
    return jnp.sum(jnp.where(pick, lengths[None, :], 0), axis=1), jnp.sum(jnp.where(pick, requests[None, :], 0), axis=1)


def reference(hidden_rows, w_query, key_matrix, value_matrix, resident_cache, page_req, req_len, assign, row_src, resident_length, page_lookup):
    scale = HEAD_SIZE ** -0.5
    share_part = QUERY_HEADS // KEY_VALUE_HEADS
    owner_list, place_list, usable_mask = jax.vmap(lambda pages: prefill_layout(pages, req_len, PAGE_TOKENS))(page_req.reshape(N_GRP, PPG))
    groups = jnp.arange(N_GRP, dtype=jnp.int32)
    prompt_length, request_item = jax.vmap(lambda sources, index: decode_layout(sources, assign, req_len, index, N_GRP))(row_src.reshape(N_GRP, DECODE_GROUPROWS), groups)
    decode_places = (prompt_length + resident_length.reshape(N_GRP, DECODE_GROUPROWS))[:, None, :] + jnp.arange(DECODE_STEPS, dtype=jnp.int32)[None, :, None]

    def project(block, where_at):
        query_rows = rotate(jnp.dot(block, w_query, preferred_element_type=jnp.float32), where_at, HEAD_SIZE).astype(jnp.bfloat16)
        key_row_block = rotate(jnp.dot(block, key_matrix, preferred_element_type=jnp.float32), where_at, HEAD_SIZE).astype(jnp.bfloat16)
        value_rows = jnp.dot(block, value_matrix, preferred_element_type=jnp.float32).astype(jnp.bfloat16)
        return query_rows.reshape(-1, QUERY_HEADS, HEAD_SIZE), key_row_block.reshape(-1, KEY_VALUE_HEADS, HEAD_SIZE), value_rows.reshape(-1, KEY_VALUE_HEADS, HEAD_SIZE)

    prefill_queries, prefill_keys, prefill_values = project(hidden_rows[0], place_list.reshape(-1))
    decoder_queries, decoder_keys, decoder_values = project(hidden_rows[1], decode_places.reshape(-1))

    def prefiller_group(inputs):
        query_rows, key_row_block, value_rows, owner, place, usable_rows = inputs
        key_full = jnp.repeat(key_row_block, share_part, axis=1).astype(jnp.float32)
        value_full = jnp.repeat(value_rows, share_part, axis=1).astype(jnp.float32)
        scores = jnp.einsum("qhd,khd->hqk", query_rows.astype(jnp.float32), key_full) * scale
        allowed = (owner[:, None] == owner[None, :]) & (place[None, :] <= place[:, None]) & usable_rows[None, :]
        allowed = allowed | jnp.eye(GROUP_ROWS, dtype=bool)
        weights = normalize(jnp.where(allowed[None], scores, masked_score))
        mixed = jnp.einsum("hqk,khd->qhd", weights.astype(jnp.float32), value_full)
        mixed = mixed * usable_rows[:, None, None].astype(jnp.float32)
        return mixed.astype(jnp.bfloat16).reshape(GROUP_ROWS, QUERY_HEADS * HEAD_SIZE)

    prefill_output = lax.map(prefiller_group, (prefill_queries.reshape(N_GRP, GROUP_ROWS, QUERY_HEADS, HEAD_SIZE), prefill_keys.reshape(N_GRP, GROUP_ROWS, KEY_VALUE_HEADS, HEAD_SIZE), prefill_values.reshape(N_GRP, GROUP_ROWS, KEY_VALUE_HEADS, HEAD_SIZE), owner_list, place_list, usable_mask)).reshape(POOL_ROWS, QUERY_HEADS * HEAD_SIZE)

    page_index = jnp.arange(N_GRP * PPG, dtype=jnp.int32)
    catalog = jnp.arange(NREQ, dtype=jnp.int32)
    first_page = jnp.min(jnp.where(page_req[None, :] == catalog[:, None], page_index[None, :], N_GRP * PPG), axis=1)
    head_lookup = (jnp.arange(N_TP, dtype=jnp.int32) // REP)[:, None] * KVN + jnp.arange(KVN, dtype=jnp.int32)[None, :]
    spans = jnp.arange(MOSTP * PAGE_TOKENS, dtype=jnp.int32)
    stored_span = ROW_PAGE_LIMIT * PAGE_TOKENS
    prompt_span = MOSTP * PAGE_TOKENS

    def decoder_group(inputs):
        query_rows, key_row_block, value_rows, cache, table, request_rows, prompt_rows, context = inputs
        grouped = query_rows.reshape(DECODE_STEPS, DECODE_GROUPROWS, N_TP, KVN, QHD // KVN, HEAD_SIZE).astype(jnp.float32)
        tokens = jnp.minimum(first_page[request_rows][:, None] * PAGE_TOKENS + spans[None, :], POOL_ROWS - 1)
        prompt_keys = prefill_keys[tokens][:, :, head_lookup].astype(jnp.float32)
        prompt_values = prefill_values[tokens][:, :, head_lookup].astype(jnp.float32)
        stored = cache[table].reshape(DECODE_GROUPROWS, stored_span, N_TP, 2, KVN, HEAD_SIZE).astype(jnp.float32)
        fresh_keys = key_row_block.reshape(DECODE_STEPS, DECODE_GROUPROWS, KEY_VALUE_HEADS, HEAD_SIZE)[:, :, head_lookup].astype(jnp.float32)
        fresh_values = value_rows.reshape(DECODE_STEPS, DECODE_GROUPROWS, KEY_VALUE_HEADS, HEAD_SIZE)[:, :, head_lookup].astype(jnp.float32)
        score_prompt = jnp.einsum("srtigd,rltid->srtigl", grouped, prompt_keys) * scale
        score_stored = jnp.einsum("srtigd,rltid->srtigl", grouped, stored[:, :, :, 0]) * scale
        score_new = jnp.einsum("srtigd,urtid->srtigu", grouped, fresh_keys) * scale
        prompt_ok = spans[None, :] < prompt_rows[:, None]
        stored_ok = jnp.arange(stored_span, dtype=jnp.int32)[None, :] < context[:, None]
        steps_ok = jnp.arange(DECODE_STEPS, dtype=jnp.int32)[None, :] <= jnp.arange(DECODE_STEPS, dtype=jnp.int32)[:, None]
        score_prompt = jnp.where(prompt_ok[None, :, None, None, None, :], score_prompt, masked_score)
        score_stored = jnp.where(stored_ok[None, :, None, None, None, :], score_stored, masked_score)
        score_new = jnp.where(steps_ok[:, None, None, None, None, :], score_new, masked_score)
        weights = normalize(jnp.concatenate([score_prompt, score_stored, score_new], axis=-1)).astype(jnp.float32)
        mixed = jnp.einsum("srtigl,rltid->srtigd", weights[..., :prompt_span], prompt_values)
        mixed = mixed + jnp.einsum("srtigl,rltid->srtigd", weights[..., prompt_span:prompt_span + stored_span], stored[:, :, :, 1])
        mixed = mixed + jnp.einsum("srtigu,urtid->srtigd", weights[..., prompt_span + stored_span:], fresh_values)
        return mixed.astype(jnp.bfloat16).reshape(DECODE_STEPS * DECODE_GROUPROWS, QUERY_HEADS * HEAD_SIZE)

    decoder_output = lax.map(decoder_group, (decoder_queries.reshape(N_GRP, GROUP_ROWS, QUERY_HEADS, HEAD_SIZE), decoder_keys.reshape(N_GRP, GROUP_ROWS, KEY_VALUE_HEADS, HEAD_SIZE), decoder_values.reshape(N_GRP, GROUP_ROWS, KEY_VALUE_HEADS, HEAD_SIZE), resident_cache.reshape(N_GRP, GROUP_PAGES, PAGE_TOKENS, CACHE_WIDTH), page_lookup.reshape(N_GRP, DECODE_GROUPROWS, ROW_PAGE_LIMIT), request_item, prompt_length, resident_length.reshape(N_GRP, DECODE_GROUPROWS))).reshape(POOL_ROWS, QUERY_HEADS * HEAD_SIZE)
    return jnp.stack([prefill_output, decoder_output])
```

```python
import functools
import math

import jax
import jax.numpy as jnp
from jax import lax
from jax.experimental import pallas as pl
from jax.experimental.pallas import tpu as pltpu
from jax.sharding import PartitionSpec as P

HEAD = 128
PAGE = 16
STEPS = 4
THETA = 500000.0
MASKED = -1e30
SCALE = HEAD**-0.5
RATE = SCALE / math.log(2.0)
KPART = 8
MODEL = 8192
KW = MODEL // KPART
RING = 8
SHARD = 64
QCOLS = 512
PIECE = KW + 256
GROUPS = 8
ROWS = 1024
DROWS = 256
HALF = 512
BIG = 63 << 20
BF = jnp.bfloat16
F32 = jnp.float32


def ring_y(step):
    return [(x * 4 + y, x * 4 + (y + step) % 4) for x in range(2) for y in range(4)]


def flip(mask):
    return [(t, t ^ mask) for t in range(16)]


def far_x():
    pairs = []
    for pool in range(2):
        for g in range(GROUPS):
            for t in range(16):
                x_hi, y = divmod(g, 4)
                x_lo, z = divmod(t, RING)
                x = x_hi * 2 + x_lo
                to = (x + 1) % 4 if x % 2 else (x - 1) % 4
                pairs.append(
                    (
                        (pool * GROUPS + g) * 16 + t,
                        (pool * GROUPS + (to // 2) * 4 + y) * 16 + (to % 2) * RING + z,
                    )
                )
    return pairs


def cut_kernel(offsets, query, key, value, *refs):
    first, second, sems = refs[-3:]
    copies = []
    for s, out in enumerate((first, second)):
        start = pl.multiple_of(offsets[s] * KW, KW)
        copies.append(
            pltpu.make_async_copy(query.at[pl.ds(start, KW), :], out.at[pl.ds(0, KW), :], sems.at[s, 0])
        )
        copies += tall_copies(key, value, start, out, sems.at[s])
    for copy in copies:
        copy.start()
    for copy in copies:
        copy.wait()


def tall_copies(key, value, start, out, sems):
    copies = []
    for run in range(2):
        for i, source in enumerate((key, value)):
            copies.append(
                pltpu.make_async_copy(
                    source.at[:, pl.ds(pl.multiple_of(start + run * QCOLS, QCOLS), QCOLS)],
                    out.at[pl.ds(KW + run * HEAD + i * SHARD, SHARD), :],
                    sems.at[1 + run * 2 + i],
                )
            )
    return copies


def cut(offsets, query, key, value, extra):
    anywhere = pl.BlockSpec(memory_space=pl.ANY)
    return pl.pallas_call(
        cut_kernel,
        out_shape=[jax.ShapeDtypeStruct((PIECE, QCOLS), BF)] * 2,
        in_specs=[pl.BlockSpec(memory_space=pltpu.SMEM)] + [anywhere] * (3 + len(extra)),
        out_specs=[pl.BlockSpec(memory_space=pltpu.VMEM)] * 2,
        scratch_shapes=[pltpu.SemaphoreType.DMA((2, 5))],
        compiler_params=pltpu.CompilerParams(vmem_limit_bytes=BIG),
        cost_estimate=pl.CostEstimate(flops=0, bytes_accessed=4 * PIECE * QCOLS * 2, transcendentals=0),
        name="cut",
    )(offsets, query, key, value, *extra)


def row_copies(order, rows, scratch, sems):
    return [
        pltpu.make_async_copy(
            rows.at[:, pl.ds(pl.multiple_of(order[k] * KW, KW), KW)], scratch.at[k], sems.at[k]
        )
        for k in range(KPART)
    ]


def tall_kernel(order, rows, key, value, *refs):
    pieces = refs[:KPART]
    own_out, side_out, xs, own_w, side_w, xsem, osem, ssem = refs[KPART:]
    x_copies = row_copies(order, rows, xs, xsem)
    copies = []
    for k in range(KPART):
        start = pl.multiple_of(order[k] * KW, KW)
        copies.append(
            [x_copies[k], pltpu.make_async_copy(pieces[k].at[pl.ds(KW, 2 * HEAD), :], side_w.at[k], ssem.at[k])]
            + [
                pltpu.make_async_copy(
                    source.at[:, pl.ds(start, KW)], own_w.at[k, pl.ds(i * SHARD, SHARD), :], osem.at[k, i]
                )
                for i, source in enumerate((key, value))
            ]
        )
        for copy in copies[k]:
            copy.start()
    dims = (((1,), (1,)), ((), ()))
    tall = None
    for k in range(KPART):
        for copy in copies[k]:
            copy.wait()
        weight = jnp.concatenate([side_w[k, :HEAD, :], side_w[k, HEAD:, :]], axis=1)
        both = lax.dot_general(
            xs[k], jnp.concatenate([own_w[k], weight], axis=0), dims, preferred_element_type=F32
        )
        tall = both if k == 0 else tall + both
    own_out[...] = tall[:, :HEAD].astype(BF)
    side_out[...] = tall[:, HEAD:].astype(BF)


def project_tall(order, rows, key, value, pieces):
    anywhere = pl.BlockSpec(memory_space=pl.ANY)
    return pl.pallas_call(
        tall_kernel,
        out_shape=[jax.ShapeDtypeStruct((HALF, HEAD), BF)] * 2,
        in_specs=[pl.BlockSpec(memory_space=pltpu.SMEM)] + [anywhere] * (3 + len(pieces)),
        out_specs=[pl.BlockSpec(memory_space=pltpu.VMEM)] * 2,
        scratch_shapes=[
            pltpu.VMEM((KPART, HALF, KW), BF),
            pltpu.VMEM((KPART, HEAD, KW), BF),
            pltpu.VMEM((KPART, 2 * HEAD, QCOLS), BF),
            pltpu.SemaphoreType.DMA((KPART,)),
            pltpu.SemaphoreType.DMA((KPART, 2)),
            pltpu.SemaphoreType.DMA((KPART,)),
        ],
        compiler_params=pltpu.CompilerParams(vmem_limit_bytes=BIG),
        cost_estimate=pl.CostEstimate(
            flops=4 * HALF * MODEL * HEAD, bytes_accessed=12 << 20, transcendentals=0
        ),
        name="project_tall",
    )(order, rows, key, value, *pieces)


def query_kernel(order, rows, *refs):
    weights = refs[:-5]
    out, xs, ws, xsem, wsem = refs[-5:]
    x_copies = row_copies(order, rows, xs, xsem)
    w_copies = []
    for k in range(KPART):
        w_copies.append(pltpu.make_async_copy(weights[k].at[pl.ds(0, KW), :], ws.at[k], wsem.at[k]))
        x_copies[k].start()
        w_copies[k].start()
    total = None
    for k in range(KPART):
        x_copies[k].wait()
        w_copies[k].wait()
        part = jnp.dot(xs[k], ws[k], preferred_element_type=F32)
        total = part if k == 0 else total + part
    out[...] = total.astype(BF)


def project_query(order, rows, weights):
    anywhere = pl.BlockSpec(memory_space=pl.ANY)
    return pl.pallas_call(
        query_kernel,
        out_shape=jax.ShapeDtypeStruct((HALF, QCOLS), BF),
        in_specs=[pl.BlockSpec(memory_space=pltpu.SMEM)] + [anywhere] * (1 + len(weights)),
        out_specs=pl.BlockSpec(memory_space=pltpu.VMEM),
        scratch_shapes=[
            pltpu.VMEM((KPART, HALF, KW), BF),
            pltpu.VMEM((KPART, KW, QCOLS), BF),
            pltpu.SemaphoreType.DMA((KPART,)),
            pltpu.SemaphoreType.DMA((KPART,)),
        ],
        compiler_params=pltpu.CompilerParams(vmem_limit_bytes=BIG),
        cost_estimate=pl.CostEstimate(
            flops=2 * HALF * MODEL * QCOLS, bytes_accessed=16 << 20, transcendentals=0
        ),
        name="project_query",
    )(order, rows, *weights)


def bring(sources, targets, sems):
    copies = [pltpu.make_async_copy(s, t, sems.at[i]) for i, (s, t) in enumerate(zip(sources, targets))]
    for copy in copies:
        copy.start()
    for copy in copies:
        copy.wait()


def swap_halves(value):
    return pltpu.roll(value, HEAD // 2, 1)


def keys_kernel(place, *refs):
    sources, (_, keys, values, bins), held, (halves, joined, sems) = refs[:6], refs[6:10], refs[10:16], refs[16:]
    own, pair, side, diag, cosine, sine = held
    bring(sources, held, sems)
    z, x_lo = place[0], place[1]
    odd = lax.rem(z, 2)
    for slot, mine, theirs in ((odd, own, side), (1 - odd, pair, diag)):
        halves[slot, pl.ds(pl.multiple_of(x_lo * HALF, HALF), HALF), :] = mine[...].astype(F32)
        halves[slot, pl.ds(pl.multiple_of((1 - x_lo) * HALF, HALF), HALF), :] = theirs[:, theirs.shape[1] - HEAD :].astype(F32)
    lower = lax.broadcasted_iota(jnp.int32, (ROWS, HEAD), 1) < HEAD // 2
    low, high = halves[0], halves[1]
    key = jnp.where(lower, low, swap_halves(high))
    value = jnp.where(lower, swap_halves(low), high).astype(BF)
    key = (key * cosine[...] + swap_halves(key) * sine[...]).astype(BF)
    keys[...] = key
    values[...] = value
    joined[pl.ds(0, ROWS), pl.ds(0, HEAD)] = key
    joined[pl.ds(0, ROWS), pl.ds(HEAD, HEAD)] = value
    joined[pl.ds(ROWS, HEAD), :] = jnp.zeros((HEAD, 2 * HEAD), BF)
    for c in range(GROUPS):
        start = pl.multiple_of(place[2 + c] * PAGE, PAGE)
        bins[c] = jnp.zeros((HEAD, 2 * HEAD), BF)
        bins[GROUPS + c] = joined[pl.ds(start, HEAD), :]


def make_keys(place, after, *arrays):
    outs = [
        jax.ShapeDtypeStruct((ROWS, HEAD), BF),
        jax.ShapeDtypeStruct((ROWS, HEAD), BF),
        jax.ShapeDtypeStruct((2 * GROUPS, HEAD, 2 * HEAD), BF),
    ]
    vm, anywhere = pl.BlockSpec(memory_space=pltpu.VMEM), pl.BlockSpec(memory_space=pl.ANY)
    return pl.pallas_call(
        keys_kernel,
        out_shape=outs,
        in_specs=[pl.BlockSpec(memory_space=pltpu.SMEM)] + [anywhere] * (len(arrays) + 1),
        out_specs=[vm] * 3,
        scratch_shapes=[
            *[pltpu.VMEM(x.shape, x.dtype) for x in arrays],
            pltpu.VMEM((2, ROWS, HEAD), F32),
            pltpu.VMEM((ROWS + HEAD, 2 * HEAD), BF),
            pltpu.SemaphoreType.DMA((len(arrays),)),
        ],
        compiler_params=pltpu.CompilerParams(vmem_limit_bytes=BIG),
        cost_estimate=pl.CostEstimate(flops=1 << 33, bytes_accessed=4 << 20, transcendentals=0),
        name="keys",
    )(place, *arrays, after)


def attend_kernel(place, lookup, order, rows, weights, *refs):
    sources, (out, acc_out, level), held, rest = refs[:9], refs[9:12], refs[12:21], refs[21:]
    xs, ws, queries, acc, fresh_k, fresh_v, xsem, wsem, sems = rest
    side, cosine, sine, keys, values, stored_bias, seen, usable, cache = held
    z, x_lo, pool = place[0], place[1], place[10]
    x_copies = row_copies(order, rows, xs, xsem)
    w_copies = [
        pltpu.make_async_copy(
            weights.at[pl.ds(pl.multiple_of(order[k] * KW, KW), KW), :], ws.at[k], wsem.at[k]
        )
        for k in range(KPART)
    ]
    copies = [pltpu.make_async_copy(sources[i], held[i], sems.at[i]) for i in range(9)]
    for k in range(KPART):
        x_copies[k].start()
        w_copies[k].start()
    for copy in copies:
        copy.start()
    own = None
    for k in range(KPART):
        x_copies[k].wait()
        w_copies[k].wait()
        part = jnp.dot(xs[k], ws[k], preferred_element_type=F32)
        own = part if k == 0 else own + part
    for copy in copies:
        copy.wait()
    for array, lo in ((own, x_lo), (side, 1 - x_lo)):
        here = pl.ds(pl.multiple_of(lo * HALF, HALF), HALF)
        c, s = cosine[here, :], sine[here, :]
        for h in range(4):
            lanes = slice(h * HEAD, (h + 1) * HEAD)
            q = array[:, lanes].astype(F32)
            q = q * c + swap_halves(q) * s
            queries[here, lanes] = q.astype(BF).astype(F32)
    dims = (((1,), (1,)), ((), ()))

    @pl.when(pool == 0)
    def _():
        fresh_k[pl.ds(0, HEAD), :] = jnp.zeros((HEAD, HEAD), F32)
        fresh_v[pl.ds(0, HEAD), :] = jnp.zeros((HEAD, HEAD), F32)
        fresh_k[pl.ds(HEAD, ROWS), :] = keys[...].astype(F32)
        fresh_v[pl.ds(HEAD, ROWS), :] = values[...].astype(F32)

        def block(b, carry):
            start = pl.multiple_of(b * HEAD, HEAD)
            k = fresh_k[pl.ds(start, 2 * HEAD), :].astype(BF)
            v = fresh_v[pl.ds(start, 2 * HEAD), :].astype(BF)
            bias = seen[b]
            keep = usable[pl.ds(start, HEAD), :]
            for h in range(4):
                q = queries[pl.ds(start, HEAD), h * HEAD : (h + 1) * HEAD].astype(BF)
                score = lax.dot_general(q, k, dims, preferred_element_type=F32) + bias
                peak = jnp.max(score, axis=1, keepdims=True)
                p = jnp.exp2((score - peak) * RATE)
                total = jnp.sum(p, axis=1, keepdims=True)
                mixed = jnp.dot(p.astype(BF), v, preferred_element_type=F32)
                out[pl.ds(start, HEAD), h * HEAD : (h + 1) * HEAD] = (mixed / total * keep).astype(BF)
            return carry

        lax.fori_loop(0, ROWS // HEAD, block, 0, unroll=2)

    @pl.when(pool == 1)
    def _():
        fresh_k[pl.ds(0, ROWS), :] = keys[...].astype(F32)
        fresh_v[pl.ds(0, ROWS), :] = values[...].astype(F32)
        out[...] = queries[...].astype(BF)
        query = lax.broadcasted_iota(jnp.int32, (HEAD, 3 * HEAD), 0)
        key = lax.broadcasted_iota(jnp.int32, (HEAD, 3 * HEAD), 1)
        row = jnp.bitwise_and(query, 7)
        step = jnp.right_shift(query, 5)
        newer = key - 2 * HEAD
        mine = (key < 2 * HEAD) & (jnp.right_shift(key, 5) == row)
        mine = mine | (
            (key >= 2 * HEAD)
            & (newer < 32)
            & (jnp.bitwise_and(newer, 7) == row)
            & (jnp.right_shift(newer, 3) <= step)
        )
        fence = jnp.where(mine, 0.0, MASKED)
        blank = jnp.zeros((96, HEAD), BF)
        quarter = jnp.right_shift(lax.broadcasted_iota(jnp.int32, (8, HEAD), 1), 5)

        def block(b, carry):
            start = pl.multiple_of(b * 8, 8)
            pages = [cache[lookup[b * 16 + i]] for i in range(16)]
            news = [pl.ds(u * DROWS + start, 8) for u in range(STEPS)]
            new_k = jnp.concatenate([fresh_k[n, :] for n in news], axis=0).astype(BF)
            new_v = jnp.concatenate([fresh_v[n, :] for n in news], axis=0).astype(BF)
            k = jnp.concatenate([page[:, :HEAD] for page in pages] + [new_k, blank], axis=0)
            v = jnp.concatenate([page[:, HEAD:] for page in pages] + [new_v, blank], axis=0)
            q = jnp.concatenate(
                [queries[n, h * HEAD : (h + 1) * HEAD] for n in news for h in range(4)], axis=0
            ).astype(BF)
            score = lax.dot_general(q, k, dims, preferred_element_type=F32)
            score = score + (fence + stored_bias[b])
            peak = jnp.max(score, axis=1, keepdims=True)
            p = jnp.exp2((score - peak) * RATE)
            total = jnp.sum(p, axis=1, keepdims=True)
            mixed = jnp.dot(p.astype(BF), v, preferred_element_type=F32) / total
            height = jnp.broadcast_to(peak + jnp.log2(total) / RATE, (HEAD, HEAD))
            for u in range(STEPS):
                lift = None
                for h in range(4):
                    at = (u * 4 + h) * 8
                    acc[news[u], h * HEAD : (h + 1) * HEAD] = mixed[at : at + 8]
                    lift = height[at : at + 8] if h == 0 else jnp.where(quarter == h, height[at : at + 8], lift)
                level[news[u], :] = lift
            return carry

        lax.fori_loop(0, DROWS // 8, block, 0, unroll=8)
        acc_out[...] = acc[...].astype(BF)


def attend(place, lookup, order, rows, weights, *arrays):
    smem, vm = pl.BlockSpec(memory_space=pltpu.SMEM), pl.BlockSpec(memory_space=pltpu.VMEM)
    return pl.pallas_call(
        attend_kernel,
        out_shape=[
            jax.ShapeDtypeStruct((ROWS, QCOLS), BF),
            jax.ShapeDtypeStruct((ROWS, QCOLS), BF),
            jax.ShapeDtypeStruct((ROWS, HEAD), F32),
        ],
        in_specs=[smem] * 3 + [pl.BlockSpec(memory_space=pl.ANY)] * (2 + len(arrays)),
        out_specs=[vm] * 3,
        scratch_shapes=[
            *[pltpu.VMEM(x.shape, x.dtype) for x in arrays],
            pltpu.VMEM((KPART, HALF, KW), BF),
            pltpu.VMEM((KPART, KW, QCOLS), BF),
            pltpu.VMEM((ROWS, QCOLS), F32),
            pltpu.VMEM((ROWS, QCOLS), F32),
            pltpu.VMEM((ROWS + HEAD, HEAD), F32),
            pltpu.VMEM((ROWS + HEAD, HEAD), F32),
            pltpu.SemaphoreType.DMA((KPART,)),
            pltpu.SemaphoreType.DMA((KPART,)),
            pltpu.SemaphoreType.DMA((len(arrays),)),
        ],
        compiler_params=pltpu.CompilerParams(vmem_limit_bytes=BIG),
        cost_estimate=pl.CostEstimate(flops=1 << 33, bytes_accessed=32 << 20, transcendentals=1 << 21),
        name="attend",
    )(place, lookup, order, rows, weights, *arrays)


def finish_kernel(place, *refs):
    sources, out, held, (masks, wide, tall_k, sems) = refs[:6], refs[6], refs[7:13], refs[13:]
    first, acc, level, arrived, source, prompt_bias = held
    pool = place[10]

    @pl.when(pool == 0)
    def _():
        bring(sources[:1], held[:1], sems)
        out[...] = first[...]

    @pl.when(pool == 1)
    def _():
        bring([*sources[:3], sources[3].at[pl.ds(0, ROWS), :], *sources[4:]], held, sems)
        dims = (((1,), (1,)), ((), ()))
        picks = source[...]
        for c in range(GROUPS):
            masks[:, c * HEAD : (c + 1) * HEAD] = jnp.where(picks == c, 1.0, 0.0).astype(BF)
            tall_k[:, c * HEAD : (c + 1) * HEAD] = arrived[c * HEAD : (c + 1) * HEAD, :HEAD]
        bias = prompt_bias[...]
        for u in range(STEPS):
            rows = slice(u * DROWS, (u + 1) * DROWS)
            for h in range(4):
                lanes = slice(h * HEAD, (h + 1) * HEAD)
                q = first[rows, lanes]
                here = slice(h * DROWS, (h + 1) * DROWS)
                for c in range(GROUPS):
                    block = slice(c * HEAD, (c + 1) * HEAD)
                    wide[here, block] = q * masks[:, block]
                score = lax.dot_general(wide[here, :], tall_k[...], dims, preferred_element_type=F32) + bias
                before = level[rows, h * 32 : h * 32 + 1]
                peak = jnp.maximum(before, jnp.max(score, axis=1, keepdims=True))
                p = jnp.exp2((score - peak) * RATE)
                fade = jnp.exp2((before - peak) * RATE)
                total = fade + jnp.sum(p, axis=1, keepdims=True)
                p = p.astype(BF)
                spread = jnp.concatenate(
                    [p * masks[:, c * HEAD : (c + 1) * HEAD] for c in range(GROUPS)], axis=1
                )
                mixed = acc[rows, lanes].astype(F32) * fade
                mixed = mixed + jnp.dot(spread, arrived[:, HEAD:], preferred_element_type=F32)
                out[rows, lanes] = (mixed / total).astype(BF)


def finish(place, *arrays):
    anywhere = pl.BlockSpec(memory_space=pl.ANY)
    held = [pltpu.VMEM(x.shape if x.shape[0] <= ROWS else (ROWS, x.shape[1]), x.dtype) for x in arrays]
    return pl.pallas_call(
        finish_kernel,
        out_shape=jax.ShapeDtypeStruct((ROWS, QCOLS), BF),
        in_specs=[pl.BlockSpec(memory_space=pltpu.SMEM)] + [anywhere] * len(arrays),
        out_specs=pl.BlockSpec(memory_space=pltpu.VMEM),
        scratch_shapes=[
            *held,
            pltpu.VMEM((DROWS, ROWS), BF),
            pltpu.VMEM((4 * DROWS, ROWS), BF),
            pltpu.VMEM((HEAD, ROWS), BF),
            pltpu.SemaphoreType.DMA((len(arrays),)),
        ],
        compiler_params=pltpu.CompilerParams(vmem_limit_bytes=BIG),
        cost_estimate=pl.CostEstimate(flops=1 << 31, bytes_accessed=8 << 20, transcendentals=1 << 20),
        name="finish",
    )(place, *arrays)


def prefill_layout(page_req, req_len):
    count = page_req.shape[0]
    index = jnp.arange(count, dtype=jnp.int32)
    same = page_req[:, None] == page_req[None, :]
    first = jnp.min(jnp.where(same, index[None, :], count), axis=1)
    owner = jnp.repeat(page_req, PAGE)
    place = jnp.arange(count * PAGE, dtype=jnp.int32) - jnp.repeat(first, PAGE) * PAGE
    match = owner[:, None] == jnp.arange(req_len.shape[0], dtype=jnp.int32)[None, :]
    lengths = jnp.sum(jnp.where(match, req_len[None, :], 0), axis=1)
    return owner, place, place < lengths


def decode_layout(row_src, assign, req_len, group):
    slots = jnp.arange(GROUPS, dtype=jnp.int32)
    table = assign.reshape(GROUPS, GROUPS)
    chosen = jnp.sum(jnp.where(table == group, slots[None, :], 0), axis=1)
    requests = slots * GROUPS + chosen
    catalog = jnp.arange(req_len.shape[0], dtype=jnp.int32)
    lengths = jnp.sum(jnp.where(requests[:, None] == catalog[None, :], req_len[None, :], 0), axis=1)
    pick = row_src[:, None] == slots[None, :]
    return jnp.sum(jnp.where(pick, lengths[None, :], 0), axis=1)


def first_pages(page_req, assign, group):
    slots = jnp.arange(GROUPS, dtype=jnp.int32)
    table = assign.reshape(GROUPS, GROUPS)
    mine = jnp.sum(jnp.where((slots == group)[:, None], table, 0), axis=0)
    local = page_req - group * GROUPS
    starts = jnp.sum((local[None, :] < slots[:, None]).astype(jnp.int32), axis=1)
    target = mine[None, :] == slots[:, None]
    return jnp.sum(jnp.where(target, starts[None, :], 0), axis=1)


def shards(
    hidden_rows,
    w_query,
    key_matrix,
    value_matrix,
    resident_cache,
    page_req,
    req_len,
    assign,
    row_src,
    resident_length,
    page_lookup,
):
    group = lax.axis_index("grp")
    tp = lax.axis_index("tp")
    pool = lax.axis_index("pool")
    y = lax.rem(group, 4)
    x_lo, z = tp // RING, lax.rem(tp, RING)
    half = lax.rem(y, 2)
    send = lambda value, axis, pairs: lax.ppermute(value, axis, pairs)

    with jax.named_scope("rows"):
        rings = [[x * RING + i for i in range(RING)] for x in range(2)]
        rows = lax.all_gather(hidden_rows[0], "tp", axis=0, tiled=True, axis_index_groups=rings)

    owner, prefill_place, usable = prefill_layout(page_req, req_len)
    prompt_length = decode_layout(row_src, assign, req_len, group)
    decode_place = (
        (prompt_length + resident_length)[None, :] + jnp.arange(STEPS, dtype=jnp.int32)[:, None]
    ).reshape(-1)
    positions = jnp.where(pool == 0, prefill_place, decode_place)
    freqs = jnp.exp(jnp.arange(HEAD // 2, dtype=F32) * (-2.0 * math.log(THETA) / HEAD))
    angles = positions.astype(F32)[:, None] * freqs[None, :]
    cosine, sine = jnp.cos(angles), jnp.sin(angles)
    cosine = jnp.concatenate([cosine, cosine], axis=1)
    sine = jnp.concatenate([-sine, sine], axis=1)
    owners = owner.reshape(GROUPS, HEAD)
    prior = jnp.concatenate([jnp.full((1, HEAD), -1, jnp.int32), owners[:-1]], axis=0)
    seen_owner = jnp.concatenate([prior, owners], axis=1)
    i = jnp.arange(HEAD, dtype=jnp.int32)[:, None]
    k = jnp.arange(2 * HEAD, dtype=jnp.int32)[None, :] - HEAD
    allowed = (owners[:, :, None] == seen_owner[:, None, :]) & (k <= i)[None]
    seen = jnp.where(allowed, 0.0, MASKED).astype(F32)
    usable_rows = jnp.broadcast_to(usable.astype(F32)[:, None], (ROWS, HEAD))
    stored_ok = jnp.arange(32, dtype=jnp.int32)[None, :] < resident_length[:, None]
    stored_bias = jnp.where(stored_ok, 0.0, MASKED).astype(F32).reshape(DROWS // 8, 1, 2 * HEAD)
    stored_bias = jnp.concatenate([stored_bias, jnp.zeros((DROWS // 8, 1, HEAD), F32)], axis=2)
    prompt_ok = jnp.arange(HEAD, dtype=jnp.int32)[None, :] < prompt_length[:, None]
    prompt_bias = jnp.where(prompt_ok, 0.0, MASKED).astype(F32)
    source = jnp.broadcast_to(row_src[:, None], (DROWS, HEAD))
    place = jnp.concatenate(
        [jnp.stack([z, x_lo]), first_pages(page_req, assign, group), pool[None]]
    ).astype(jnp.int32)
    lookup = page_lookup.reshape(-1)
    tables = (cosine, sine, seen, usable_rows, stored_bias, prompt_bias, source, place, lookup)

    with jax.named_scope("weights"):
        own_weight = (w_query, key_matrix.T, value_matrix.T)
        offsets = jnp.stack([half * 4 + pool, half * 4 + 2 + pool]).astype(jnp.int32)
        piece0, piece1 = cut(offsets, *own_weight, tables)
        swap_core = [(0, 1), (1, 0)]
        a0 = send(piece0, "tp", flip(8))
        a1 = send(piece1, ("pool", "grp", "tp"), far_x())
        b0 = send(a0, "grp", ring_y(-1))
        b1 = send(a1, "grp", ring_y(1))
        parts = [a0, a1, b0, b1] + [send(v, "pool", swap_core) for v in (a0, a1, b0, b1)]
        order = []
        for h, p in ((half, pool), (1 - half, pool), (half, 1 - pool), (1 - half, 1 - pool)):
            order += [h * 4 + p, h * 4 + 2 + p]
        order = jnp.stack(order).astype(jnp.int32)

    own_kv, side_kv = project_tall(order, rows, own_weight[1], own_weight[2], parts)
    pair = send(own_kv, "tp", flip(1))
    side = send(side_kv, "tp", flip(8))
    diag = send(side_kv, "tp", flip(9))
    other_query = project_query(order, rows, parts)
    side_query = send(other_query, "tp", flip(8))
    keys, values, bins = make_keys(place, other_query, own_kv, pair, side, diag, cosine, sine)
    arrived = lax.all_to_all(bins, ("pool", "grp"), split_axis=0, concat_axis=0, tiled=True)
    first, acc, level = attend(
        place,
        lookup,
        order,
        rows,
        w_query,
        side_query,
        cosine,
        sine,
        keys,
        values,
        stored_bias,
        seen,
        usable_rows,
        resident_cache,
    )
    return finish(
        place, first, acc, level, arrived.reshape(2 * ROWS, 2 * HEAD), source, prompt_bias
    )[None]


def solution(mesh):
    return jax.shard_map(
        shards,
        mesh=mesh,
        in_specs=(
            P("pool", ("grp", "tp"), None),
            P(None, "tp"),
            P(None, "tp"),
            P(None, "tp"),
            P("grp", None, "tp"),
            P("grp"),
            P(),
            P(),
            P("grp"),
            P("grp"),
            P("grp", None),
        ),
        out_specs=P("pool", "grp", "tp"),
        check_vma=False,
    )
```

```python
import functools
import math

import jax
import jax.numpy as jnp
from jax import lax
from jax.experimental import pallas as pl
from jax.experimental.pallas import tpu as pltpu
from jax.sharding import PartitionSpec as P

HEAD = 128
PAGE = 16
STEPS = 4
THETA = 500000.0
MASKED = -1e30
SCALE = HEAD**-0.5
RATE = SCALE / math.log(2.0)
KPART = 8
MODEL = 8192
KW = MODEL // KPART
RING = 8
SHARD = 64
QCOLS = 512
PIECE = KW + 256
GROUPS = 8
ROWS = 1024
DROWS = 256
HALF = 512
BIG = (64 << 20) - (192 << 10)
BF = jnp.bfloat16
F32 = jnp.float32


def ring_y(step):
    return [(x * 4 + y, x * 4 + (y + step) % 4) for x in range(2) for y in range(4)]


def flip(mask):
    return [(t, t ^ mask) for t in range(16)]


def far_x():
    pairs = []
    for pool in range(2):
        for g in range(GROUPS):
            for t in range(16):
                x_hi, y = divmod(g, 4)
                x_lo, z = divmod(t, RING)
                x = x_hi * 2 + x_lo
                to = (x + 1) % 4 if x % 2 else (x - 1) % 4
                pairs.append(
                    (
                        (pool * GROUPS + g) * 16 + t,
                        (pool * GROUPS + (to // 2) * 4 + y) * 16 + (to % 2) * RING + z,
                    )
                )
    return pairs


def cut_kernel(offsets, query, key, value, *refs):
    first, second, sems = refs[-3:]
    copies = []
    for s, out in enumerate((first, second)):
        start = pl.multiple_of(offsets[s] * KW, KW)
        copies.append(
            pltpu.make_async_copy(query.at[pl.ds(start, KW), :], out.at[pl.ds(0, KW), :], sems.at[s, 0])
        )
        copies += tall_copies(key, value, start, out, sems.at[s])
    for copy in copies:
        copy.start()
    for copy in copies:
        copy.wait()


def tall_copies(key, value, start, out, sems):
    copies = []
    for run in range(2):
        for i, source in enumerate((key, value)):
            copies.append(
                pltpu.make_async_copy(
                    source.at[:, pl.ds(pl.multiple_of(start + run * QCOLS, QCOLS), QCOLS)],
                    out.at[pl.ds(KW + run * HEAD + i * SHARD, SHARD), :],
                    sems.at[1 + run * 2 + i],
                )
            )
    return copies


def cut(offsets, query, key, value, extra):
    anywhere = pl.BlockSpec(memory_space=pl.ANY)
    return pl.pallas_call(
        cut_kernel,
        out_shape=[jax.ShapeDtypeStruct((PIECE, QCOLS), BF)] * 2,
        in_specs=[pl.BlockSpec(memory_space=pltpu.SMEM)] + [anywhere] * (3 + len(extra)),
        out_specs=[pl.BlockSpec(memory_space=pltpu.VMEM)] * 2,
        scratch_shapes=[pltpu.SemaphoreType.DMA((2, 5))],
        compiler_params=pltpu.CompilerParams(vmem_limit_bytes=BIG),
        cost_estimate=pl.CostEstimate(flops=0, bytes_accessed=4 * PIECE * QCOLS * 2, transcendentals=0),
        name="cut",
    )(offsets, query, key, value, *extra)


def row_copies(order, rows, scratch, sems):
    return [
        pltpu.make_async_copy(
            rows.at[:, pl.ds(pl.multiple_of(order[k] * KW, KW), KW)], scratch.at[k], sems.at[k]
        )
        for k in range(KPART)
    ]


def tall_kernel(order, rows, key, value, *refs):
    pieces = refs[:KPART]
    own_out, side_out, xs, own_w, side_w, xsem, osem, ssem = refs[KPART:]
    x_copies = row_copies(order, rows, xs, xsem)
    copies = []
    for k in range(KPART):
        start = pl.multiple_of(order[k] * KW, KW)
        copies.append(
            [x_copies[k], pltpu.make_async_copy(pieces[k].at[pl.ds(KW, 2 * HEAD), :], side_w.at[k], ssem.at[k])]
            + [
                pltpu.make_async_copy(
                    source.at[:, pl.ds(start, KW)], own_w.at[k, pl.ds(i * SHARD, SHARD), :], osem.at[k, i]
                )
                for i, source in enumerate((key, value))
            ]
        )
        for copy in copies[k]:
            copy.start()
    dims = (((1,), (1,)), ((), ()))
    tall = None
    for k in range(KPART):
        for copy in copies[k]:
            copy.wait()
        weight = jnp.concatenate([side_w[k, :HEAD, :], side_w[k, HEAD:, :]], axis=1)
        both = lax.dot_general(
            xs[k], jnp.concatenate([own_w[k], weight], axis=0), dims, preferred_element_type=F32
        )
        tall = both if k == 0 else tall + both
    own_out[...] = tall[:, :HEAD].astype(BF)
    side_out[...] = tall[:, HEAD:].astype(BF)


def project_tall(order, rows, key, value, pieces):
    anywhere = pl.BlockSpec(memory_space=pl.ANY)
    return pl.pallas_call(
        tall_kernel,
        out_shape=[jax.ShapeDtypeStruct((HALF, HEAD), BF)] * 2,
        in_specs=[pl.BlockSpec(memory_space=pltpu.SMEM)] + [anywhere] * (3 + len(pieces)),
        out_specs=[pl.BlockSpec(memory_space=pltpu.VMEM)] * 2,
        scratch_shapes=[
            pltpu.VMEM((KPART, HALF, KW), BF),
            pltpu.VMEM((KPART, HEAD, KW), BF),
            pltpu.VMEM((KPART, 2 * HEAD, QCOLS), BF),
            pltpu.SemaphoreType.DMA((KPART,)),
            pltpu.SemaphoreType.DMA((KPART, 2)),
            pltpu.SemaphoreType.DMA((KPART,)),
        ],
        compiler_params=pltpu.CompilerParams(vmem_limit_bytes=BIG),
        cost_estimate=pl.CostEstimate(
            flops=4 * HALF * MODEL * HEAD, bytes_accessed=12 << 20, transcendentals=0
        ),
        name="project_tall",
    )(order, rows, key, value, *pieces)


def query_kernel(order, rows, *refs):
    weights = refs[:-5]
    out, xs, ws, xsem, wsem = refs[-5:]
    x_copies = row_copies(order, rows, xs, xsem)
    w_copies = []
    for k in range(KPART):
        w_copies.append(pltpu.make_async_copy(weights[k].at[pl.ds(0, KW), :], ws.at[k], wsem.at[k]))
        x_copies[k].start()
        w_copies[k].start()
    total = None
    for k in range(KPART):
        x_copies[k].wait()
        w_copies[k].wait()
        part = jnp.dot(xs[k], ws[k], preferred_element_type=F32)
        total = part if k == 0 else total + part
    out[...] = total.astype(BF)


def project_query(order, rows, weights):
    anywhere = pl.BlockSpec(memory_space=pl.ANY)
    return pl.pallas_call(
        query_kernel,
        out_shape=jax.ShapeDtypeStruct((HALF, QCOLS), BF),
        in_specs=[pl.BlockSpec(memory_space=pltpu.SMEM)] + [anywhere] * (1 + len(weights)),
        out_specs=pl.BlockSpec(memory_space=pltpu.VMEM),
        scratch_shapes=[
            pltpu.VMEM((KPART, HALF, KW), BF),
            pltpu.VMEM((KPART, KW, QCOLS), BF),
            pltpu.SemaphoreType.DMA((KPART,)),
            pltpu.SemaphoreType.DMA((KPART,)),
        ],
        compiler_params=pltpu.CompilerParams(vmem_limit_bytes=BIG),
        cost_estimate=pl.CostEstimate(
            flops=2 * HALF * MODEL * QCOLS, bytes_accessed=16 << 20, transcendentals=0
        ),
        name="project_query",
    )(order, rows, *weights)


def bring(sources, targets, sems):
    copies = [pltpu.make_async_copy(s, t, sems.at[i]) for i, (s, t) in enumerate(zip(sources, targets))]
    for copy in copies:
        copy.start()
    for copy in copies:
        copy.wait()


def swap_halves(value):
    return pltpu.roll(value, HEAD // 2, 1)


def keys_kernel(place, *refs):
    sources, (_, keys, values, bins), held, (halves, joined, sems) = refs[:6], refs[6:10], refs[10:16], refs[16:]
    own, pair, side, diag, cosine, sine = held
    bring(sources, held, sems)
    z, x_lo = place[0], place[1]
    odd = lax.rem(z, 2)
    for slot, mine, theirs in ((odd, own, side), (1 - odd, pair, diag)):
        halves[slot, pl.ds(pl.multiple_of(x_lo * HALF, HALF), HALF), :] = mine[...].astype(F32)
        halves[slot, pl.ds(pl.multiple_of((1 - x_lo) * HALF, HALF), HALF), :] = theirs[:, theirs.shape[1] - HEAD :].astype(F32)
    lower = lax.broadcasted_iota(jnp.int32, (ROWS, HEAD), 1) < HEAD // 2
    low, high = halves[0], halves[1]
    key = jnp.where(lower, low, swap_halves(high))
    value = jnp.where(lower, swap_halves(low), high).astype(BF)
    key = (key * cosine[...] + swap_halves(key) * sine[...]).astype(BF)
    keys[...] = key
    values[...] = value
    joined[pl.ds(0, ROWS), pl.ds(0, HEAD)] = key
    joined[pl.ds(0, ROWS), pl.ds(HEAD, HEAD)] = value
    joined[pl.ds(ROWS, HEAD), :] = jnp.zeros((HEAD, 2 * HEAD), BF)
    for c in range(GROUPS):
        start = pl.multiple_of(place[2 + c] * PAGE, PAGE)
        bins[c] = jnp.zeros((HEAD, 2 * HEAD), BF)
        bins[GROUPS + c] = joined[pl.ds(start, HEAD), :]


def make_keys(place, after, *arrays):
    outs = [
        jax.ShapeDtypeStruct((ROWS, HEAD), BF),
        jax.ShapeDtypeStruct((ROWS, HEAD), BF),
        jax.ShapeDtypeStruct((2 * GROUPS, HEAD, 2 * HEAD), BF),
    ]
    vm, anywhere = pl.BlockSpec(memory_space=pltpu.VMEM), pl.BlockSpec(memory_space=pl.ANY)
    return pl.pallas_call(
        keys_kernel,
        out_shape=outs,
        in_specs=[pl.BlockSpec(memory_space=pltpu.SMEM)] + [anywhere] * (len(arrays) + 1),
        out_specs=[vm] * 3,
        scratch_shapes=[
            *[pltpu.VMEM(x.shape, x.dtype) for x in arrays],
            pltpu.VMEM((2, ROWS, HEAD), F32),
            pltpu.VMEM((ROWS + HEAD, 2 * HEAD), BF),
            pltpu.SemaphoreType.DMA((len(arrays),)),
        ],
        compiler_params=pltpu.CompilerParams(vmem_limit_bytes=BIG),
        cost_estimate=pl.CostEstimate(flops=1 << 33, bytes_accessed=4 << 20, transcendentals=0),
        name="keys",
    )(place, *arrays, after)


def attend_kernel(place, lookup, order, rows, weights, *refs):
    sources, (out, acc_out, level), held, rest = refs[:9], refs[9:12], refs[12:21], refs[21:]
    xs, ws, queries, acc, fresh_k, fresh_v, xsem, wsem, sems = rest
    side, cosine, sine, keys, values, stored_bias, seen, usable, cache = held
    z, x_lo, pool = place[0], place[1], place[10]
    x_copies = row_copies(order, rows, xs, xsem)
    w_copies = [
        pltpu.make_async_copy(
            weights.at[pl.ds(pl.multiple_of(order[k] * KW, KW), KW), :], ws.at[k], wsem.at[k]
        )
        for k in range(KPART)
    ]
    copies = [pltpu.make_async_copy(sources[i], held[i], sems.at[i]) for i in range(9)]
    for k in range(KPART):
        x_copies[k].start()
        w_copies[k].start()
    for copy in copies:
        copy.start()
    own = None
    for k in range(KPART):
        x_copies[k].wait()
        w_copies[k].wait()
        part = jnp.dot(xs[k], ws[k], preferred_element_type=F32)
        own = part if k == 0 else own + part
    for copy in copies:
        copy.wait()
    for array, lo in ((own, x_lo), (side, 1 - x_lo)):
        here = pl.ds(pl.multiple_of(lo * HALF, HALF), HALF)
        c, s = cosine[here, :], sine[here, :]
        for h in range(4):
            lanes = slice(h * HEAD, (h + 1) * HEAD)
            q = array[:, lanes].astype(F32)
            q = q * c + swap_halves(q) * s
            queries[here, lanes] = q.astype(BF).astype(F32)
    dims = (((1,), (1,)), ((), ()))

    @pl.when(pool == 0)
    def _():
        fresh_k[pl.ds(0, HEAD), :] = jnp.zeros((HEAD, HEAD), F32)
        fresh_v[pl.ds(0, HEAD), :] = jnp.zeros((HEAD, HEAD), F32)
        fresh_k[pl.ds(HEAD, ROWS), :] = keys[...].astype(F32)
        fresh_v[pl.ds(HEAD, ROWS), :] = values[...].astype(F32)

        def block(b, carry):
            start = pl.multiple_of(b * HEAD, HEAD)
            k = fresh_k[pl.ds(start, 2 * HEAD), :].astype(BF)
            v = fresh_v[pl.ds(start, 2 * HEAD), :].astype(BF)
            bias = seen[b]
            keep = usable[pl.ds(start, HEAD), :]
            for h in range(4):
                q = queries[pl.ds(start, HEAD), h * HEAD : (h + 1) * HEAD].astype(BF)
                score = lax.dot_general(q, k, dims, preferred_element_type=F32) + bias
                peak = jnp.max(score, axis=1, keepdims=True)
                p = jnp.exp2((score - peak) * RATE)
                total = jnp.sum(p, axis=1, keepdims=True)
                mixed = jnp.dot(p.astype(BF), v, preferred_element_type=F32)
                out[pl.ds(start, HEAD), h * HEAD : (h + 1) * HEAD] = (mixed / total * keep).astype(BF)
            return carry

        lax.fori_loop(0, ROWS // HEAD, block, 0, unroll=2)

    @pl.when(pool == 1)
    def _():
        fresh_k[pl.ds(0, ROWS), :] = keys[...].astype(F32)
        fresh_v[pl.ds(0, ROWS), :] = values[...].astype(F32)
        out[...] = queries[...].astype(BF)
        query = lax.broadcasted_iota(jnp.int32, (HEAD, 3 * HEAD), 0)
        key = lax.broadcasted_iota(jnp.int32, (HEAD, 3 * HEAD), 1)
        row = jnp.bitwise_and(query, 7)
        step = jnp.right_shift(query, 5)
        newer = key - 2 * HEAD
        mine = (key < 2 * HEAD) & (jnp.right_shift(key, 5) == row)
        mine = mine | (
            (key >= 2 * HEAD)
            & (newer < 32)
            & (jnp.bitwise_and(newer, 7) == row)
            & (jnp.right_shift(newer, 3) <= step)
        )
        fence = jnp.where(mine, 0.0, MASKED)
        blank = jnp.zeros((96, HEAD), BF)
        quarter = jnp.right_shift(lax.broadcasted_iota(jnp.int32, (8, HEAD), 1), 5)

        def block(b, carry):
            start = pl.multiple_of(b * 8, 8)
            pages = [cache[lookup[b * 16 + i]] for i in range(16)]
            news = [pl.ds(u * DROWS + start, 8) for u in range(STEPS)]
            new_k = jnp.concatenate([fresh_k[n, :] for n in news], axis=0).astype(BF)
            new_v = jnp.concatenate([fresh_v[n, :] for n in news], axis=0).astype(BF)
            k = jnp.concatenate([page[:, :HEAD] for page in pages] + [new_k, blank], axis=0)
            v = jnp.concatenate([page[:, HEAD:] for page in pages] + [new_v, blank], axis=0)
            q = jnp.concatenate(
                [queries[n, h * HEAD : (h + 1) * HEAD] for n in news for h in range(4)], axis=0
            ).astype(BF)
            score = lax.dot_general(q, k, dims, preferred_element_type=F32)
            score = score + (fence + stored_bias[b])
            peak = jnp.max(score, axis=1, keepdims=True)
            p = jnp.exp2((score - peak) * RATE)
            total = jnp.sum(p, axis=1, keepdims=True)
            mixed = jnp.dot(p.astype(BF), v, preferred_element_type=F32) / total
            height = jnp.broadcast_to(peak + jnp.log2(total) / RATE, (HEAD, HEAD))
            for u in range(STEPS):
                lift = None
                for h in range(4):
                    at = (u * 4 + h) * 8
                    acc[news[u], h * HEAD : (h + 1) * HEAD] = mixed[at : at + 8]
                    lift = height[at : at + 8] if h == 0 else jnp.where(quarter == h, height[at : at + 8], lift)
                level[news[u], :] = lift
            return carry

        lax.fori_loop(0, DROWS // 8, block, 0, unroll=16)
        acc_out[...] = acc[...].astype(BF)


def attend(place, lookup, order, rows, weights, *arrays):
    smem, vm = pl.BlockSpec(memory_space=pltpu.SMEM), pl.BlockSpec(memory_space=pltpu.VMEM)
    return pl.pallas_call(
        attend_kernel,
        out_shape=[
            jax.ShapeDtypeStruct((ROWS, QCOLS), BF),
            jax.ShapeDtypeStruct((ROWS, QCOLS), BF),
            jax.ShapeDtypeStruct((ROWS, HEAD), F32),
        ],
        in_specs=[smem] * 3 + [pl.BlockSpec(memory_space=pl.ANY)] * (2 + len(arrays)),
        out_specs=[vm] * 3,
        scratch_shapes=[
            *[pltpu.VMEM(x.shape, x.dtype) for x in arrays],
            pltpu.VMEM((KPART, HALF, KW), BF),
            pltpu.VMEM((KPART, KW, QCOLS), BF),
            pltpu.VMEM((ROWS, QCOLS), F32),
            pltpu.VMEM((ROWS, QCOLS), F32),
            pltpu.VMEM((ROWS + HEAD, HEAD), F32),
            pltpu.VMEM((ROWS + HEAD, HEAD), F32),
            pltpu.SemaphoreType.DMA((KPART,)),
            pltpu.SemaphoreType.DMA((KPART,)),
            pltpu.SemaphoreType.DMA((len(arrays),)),
        ],
        compiler_params=pltpu.CompilerParams(vmem_limit_bytes=BIG),
        cost_estimate=pl.CostEstimate(flops=1 << 33, bytes_accessed=32 << 20, transcendentals=1 << 21),
        name="attend",
    )(place, lookup, order, rows, weights, *arrays)


def finish_kernel(place, *refs):
    sources, out, held, (whole, masks, tall_k, sems, osems) = refs[:6], refs[6], refs[7:13], refs[13:]
    first, acc, level, arrived, source, prompt_bias = held
    pool = place[10]

    @pl.when(pool == 0)
    def _():
        bring(sources[:1], held[:1], sems)
        copy = pltpu.make_async_copy(first, out, osems.at[0])
        copy.start()
        copy.wait()

    @pl.when(pool == 1)
    def _():
        sources_here = [*sources[:3], sources[3].at[pl.ds(0, ROWS), :], *sources[4:]]
        copies = [pltpu.make_async_copy(sources_here[i], held[i], sems.at[i]) for i in range(6)]
        for i in (4, 3, 5, 0, 2, 1):
            copies[i].start()
        dims = (((1,), (1,)), ((), ()))
        copies[4].wait()
        copies[3].wait()
        picks = source[...]
        for c in range(GROUPS):
            masks[:, c * HEAD : (c + 1) * HEAD] = jnp.where(picks == c, 1.0, 0.0).astype(BF)
            tall_k[:, c * HEAD : (c + 1) * HEAD] = arrived[c * HEAD : (c + 1) * HEAD, :HEAD]
        for i in (5, 0, 2, 1):
            copies[i].wait()
        sent = [
            pltpu.make_async_copy(
                whole.at[pl.ds(u * DROWS, DROWS), :], out.at[pl.ds(u * DROWS, DROWS), :], osems.at[u]
            )
            for u in range(STEPS)
        ]
        bias = prompt_bias[...]
        for u in range(STEPS):
            rows = slice(u * DROWS, (u + 1) * DROWS)
            for h in range(4):
                lanes = slice(h * HEAD, (h + 1) * HEAD)
                q = first[rows, lanes]
                spread = jnp.concatenate(
                    [q * masks[:, c * HEAD : (c + 1) * HEAD] for c in range(GROUPS)], axis=1
                )
                score = lax.dot_general(spread, tall_k[...], dims, preferred_element_type=F32) + bias
                before = level[rows, h * 32 : h * 32 + 1]
                peak = jnp.maximum(before, jnp.max(score, axis=1, keepdims=True))
                p = jnp.exp2((score - peak) * RATE)
                fade = jnp.exp2((before - peak) * RATE)
                total = fade + jnp.sum(p, axis=1, keepdims=True)
                p = p.astype(BF)
                spread = jnp.concatenate(
                    [p * masks[:, c * HEAD : (c + 1) * HEAD] for c in range(GROUPS)], axis=1
                )
                mixed = acc[rows, lanes].astype(F32) * fade
                mixed = mixed + jnp.dot(spread, arrived[:, HEAD:], preferred_element_type=F32)
                whole[rows, lanes] = (mixed / total).astype(BF)
            sent[u].start()
        for copy in sent:
            copy.wait()


def finish(place, *arrays):
    anywhere = pl.BlockSpec(memory_space=pl.ANY)
    held = [pltpu.VMEM(x.shape if x.shape[0] <= ROWS else (ROWS, x.shape[1]), x.dtype) for x in arrays]
    return pl.pallas_call(
        finish_kernel,
        out_shape=jax.ShapeDtypeStruct((ROWS, QCOLS), BF),
        in_specs=[pl.BlockSpec(memory_space=pltpu.SMEM)] + [anywhere] * len(arrays),
        out_specs=anywhere,
        scratch_shapes=[
            *held,
            pltpu.VMEM((ROWS, QCOLS), BF),
            pltpu.VMEM((DROWS, ROWS), BF),
            pltpu.VMEM((HEAD, ROWS), BF),
            pltpu.SemaphoreType.DMA((len(arrays),)),
            pltpu.SemaphoreType.DMA((STEPS,)),
        ],
        compiler_params=pltpu.CompilerParams(vmem_limit_bytes=BIG),
        cost_estimate=pl.CostEstimate(flops=1 << 31, bytes_accessed=8 << 20, transcendentals=1 << 20),
        name="finish",
    )(place, *arrays)


def prefill_layout(page_req, req_len):
    count = page_req.shape[0]
    index = jnp.arange(count, dtype=jnp.int32)
    same = page_req[:, None] == page_req[None, :]
    first = jnp.min(jnp.where(same, index[None, :], count), axis=1)
    owner = jnp.repeat(page_req, PAGE)
    place = jnp.arange(count * PAGE, dtype=jnp.int32) - jnp.repeat(first, PAGE) * PAGE
    match = owner[:, None] == jnp.arange(req_len.shape[0], dtype=jnp.int32)[None, :]
    lengths = jnp.sum(jnp.where(match, req_len[None, :], 0), axis=1)
    return owner, place, place < lengths


def decode_layout(row_src, assign, req_len, group):
    slots = jnp.arange(GROUPS, dtype=jnp.int32)
    table = assign.reshape(GROUPS, GROUPS)
    chosen = jnp.sum(jnp.where(table == group, slots[None, :], 0), axis=1)
    requests = slots * GROUPS + chosen
    catalog = jnp.arange(req_len.shape[0], dtype=jnp.int32)
    lengths = jnp.sum(jnp.where(requests[:, None] == catalog[None, :], req_len[None, :], 0), axis=1)
    pick = row_src[:, None] == slots[None, :]
    return jnp.sum(jnp.where(pick, lengths[None, :], 0), axis=1)


def first_pages(page_req, assign, group):
    slots = jnp.arange(GROUPS, dtype=jnp.int32)
    table = assign.reshape(GROUPS, GROUPS)
    mine = jnp.sum(jnp.where((slots == group)[:, None], table, 0), axis=0)
    local = page_req - group * GROUPS
    starts = jnp.sum((local[None, :] < slots[:, None]).astype(jnp.int32), axis=1)
    target = mine[None, :] == slots[:, None]
    return jnp.sum(jnp.where(target, starts[None, :], 0), axis=1)


def shards(
    hidden_rows,
    w_query,
    key_matrix,
    value_matrix,
    resident_cache,
    page_req,
    req_len,
    assign,
    row_src,
    resident_length,
    page_lookup,
):
    group = lax.axis_index("grp")
    tp = lax.axis_index("tp")
    pool = lax.axis_index("pool")
    y = lax.rem(group, 4)
    x_lo, z = tp // RING, lax.rem(tp, RING)
    half = lax.rem(y, 2)
    send = lambda value, axis, pairs: lax.ppermute(value, axis, pairs)

    with jax.named_scope("rows"):
        rings = [[x * RING + i for i in range(RING)] for x in range(2)]
        rows = lax.all_gather(hidden_rows[0], "tp", axis=0, tiled=True, axis_index_groups=rings)

    owner, prefill_place, usable = prefill_layout(page_req, req_len)
    prompt_length = decode_layout(row_src, assign, req_len, group)
    decode_place = (
        (prompt_length + resident_length)[None, :] + jnp.arange(STEPS, dtype=jnp.int32)[:, None]
    ).reshape(-1)
    positions = jnp.where(pool == 0, prefill_place, decode_place)
    freqs = jnp.exp(jnp.arange(HEAD // 2, dtype=F32) * (-2.0 * math.log(THETA) / HEAD))
    angles = positions.astype(F32)[:, None] * freqs[None, :]
    cosine, sine = jnp.cos(angles), jnp.sin(angles)
    cosine = jnp.concatenate([cosine, cosine], axis=1)
    sine = jnp.concatenate([-sine, sine], axis=1)
    owners = owner.reshape(GROUPS, HEAD)
    prior = jnp.concatenate([jnp.full((1, HEAD), -1, jnp.int32), owners[:-1]], axis=0)
    seen_owner = jnp.concatenate([prior, owners], axis=1)
    i = jnp.arange(HEAD, dtype=jnp.int32)[:, None]
    k = jnp.arange(2 * HEAD, dtype=jnp.int32)[None, :] - HEAD
    allowed = (owners[:, :, None] == seen_owner[:, None, :]) & (k <= i)[None]
    seen = jnp.where(allowed, 0.0, MASKED).astype(F32)
    usable_rows = jnp.broadcast_to(usable.astype(F32)[:, None], (ROWS, HEAD))
    stored_ok = jnp.arange(32, dtype=jnp.int32)[None, :] < resident_length[:, None]
    stored_bias = jnp.where(stored_ok, 0.0, MASKED).astype(F32).reshape(DROWS // 8, 1, 2 * HEAD)
    stored_bias = jnp.concatenate([stored_bias, jnp.zeros((DROWS // 8, 1, HEAD), F32)], axis=2)
    prompt_ok = jnp.arange(HEAD, dtype=jnp.int32)[None, :] < prompt_length[:, None]
    prompt_bias = jnp.where(prompt_ok, 0.0, MASKED).astype(F32)
    source = jnp.broadcast_to(row_src[:, None], (DROWS, HEAD))
    place = jnp.concatenate(
        [jnp.stack([z, x_lo]), first_pages(page_req, assign, group), pool[None]]
    ).astype(jnp.int32)
    lookup = page_lookup.reshape(-1)
    tables = (cosine, sine, seen, usable_rows, stored_bias, prompt_bias, source, place, lookup)

    with jax.named_scope("weights"):
        own_weight = (w_query, key_matrix.T, value_matrix.T)
        offsets = jnp.stack([half * 4 + pool, half * 4 + 2 + pool]).astype(jnp.int32)
        piece0, piece1 = cut(offsets, *own_weight, tables)
        swap_core = [(0, 1), (1, 0)]
        a0 = send(piece0, "tp", flip(8))
        a1 = send(piece1, ("pool", "grp", "tp"), far_x())
        b0 = send(a0, "grp", ring_y(-1))
        b1 = send(a1, "grp", ring_y(1))
        parts = [a0, a1, b0, b1] + [send(v, "pool", swap_core) for v in (a0, a1, b0, b1)]
        order = []
        for h, p in ((half, pool), (1 - half, pool), (half, 1 - pool), (1 - half, 1 - pool)):
            order += [h * 4 + p, h * 4 + 2 + p]
        order = jnp.stack(order).astype(jnp.int32)

    own_kv, side_kv = project_tall(order, rows, own_weight[1], own_weight[2], parts)
    pair = send(own_kv, "tp", flip(1))
    side = send(side_kv, "tp", flip(8))
    diag = send(side_kv, "tp", flip(9))
    other_query = project_query(order, rows, parts)
    side_query = send(other_query, "tp", flip(8))
    keys, values, bins = make_keys(place, other_query, own_kv, pair, side, diag, cosine, sine)
    arrived = lax.all_to_all(bins, ("pool", "grp"), split_axis=0, concat_axis=0, tiled=True)
    first, acc, level = attend(
        place,
        lookup,
        order,
        rows,
        w_query,
        side_query,
        cosine,
        sine,
        keys,
        values,
        stored_bias,
        seen,
        usable_rows,
        resident_cache,
    )
    return finish(
        place, first, acc, level, arrived.reshape(2 * ROWS, 2 * HEAD), source, prompt_bias
    )[None]


def solution(mesh):
    return jax.shard_map(
        shards,
        mesh=mesh,
        in_specs=(
            P("pool", ("grp", "tp"), None),
            P(None, "tp"),
            P(None, "tp"),
            P(None, "tp"),
            P("grp", None, "tp"),
            P("grp"),
            P(),
            P(),
            P("grp"),
            P("grp"),
            P("grp", None),
        ),
        out_specs=P("pool", "grp", "tp"),
        check_vma=False,
    )
```
